32 devices in a mesh: grp: 2 (over core), row: 8 (over z, y), col: 2 (over x).
Axes of the slice: x: 2, y: 2, z: 4, core: 2. Of those that a mesh axis runs over, the one named last changes fastest.
Arguments:
- kkt: float32 [16384, 16384], P('row', ('grp', 'col')), as said below
- directions: float32 [16384, 2048], P('row', ('grp', 'col')), may hold values from -6 to 6
Outputs:
- schur: float32 [16384, 16384], P('row', ('grp', 'col'))
- solved: float32 [16384, 2048], P('row', ('grp', 'col'))
The draws below stay inside these ranges and needn't reach their ends.
Inputs may be any that keep to these rules, and one draw needn't show every extreme that they name: `kkt`: symmetric and positive definite, every eigenvalue at least 0.5.
All inputs are finite; a program needn't handle non-finite values.
Results may differ from the reference program's by a relative error of at most 0.0001.
Values sent between devices are 32-bit elements; how exact they have to be, the bound alone decides.
A program may use at most 256 MiB of HBM per device.

```python
import math
import jax
import jax.numpy as jnp
from jax import lax

N = 16384
M = 2048
NB = 128
PANELS = 3
STRIDE = 4096


kernel_reach = 0.15


def draw_kkt(key, part):
    base = jax.random.fold_in(key, 17)
    key_position, key_scaling, key_extra = jax.random.split(base, 3)
    position = jax.random.uniform(key_position, (N, 3), jnp.float32)
    scaling = jax.random.uniform(key_scaling, (N,), jnp.float32, 0.5, 1.5)
    extra = jax.random.uniform(key_extra, (N,), jnp.float32, 0.5, 2.0)
    distance = jnp.abs(position[:, None, 0] - position[None, :, 0])
    distance = distance + jnp.abs(position[:, None, 1] - position[None, :, 1])
    distance = distance + jnp.abs(position[:, None, 2] - position[None, :, 2])
    kernel = jnp.exp(-distance / kernel_reach)
    matrix = scaling[:, None] * scaling[None, :] * kernel
    indices = jnp.arange(N, dtype=jnp.int32)
    matrix = matrix + jnp.where(indices[:, None] == indices[None, :], extra[:, None], 0.0)
    return matrix.astype(jnp.float32)


def level_of(rng, dims, shards, low, top_value):
    factor_of = 1.0
    for dim, shards_of in shards:
        steps = jax.random.uniform(jax.random.fold_in(jax.random.fold_in(rng, 6), dim), (shards_of,), jnp.float32, low / len(shards), top_value / len(shards))
        factor_of = factor_of * jnp.repeat(jnp.exp(steps), dims[dim] // shards_of).reshape((-1,) + (1,) * (len(dims) - 1 - dim))
    return factor_of


def gaussian(rng, extent, spread, bound, cuts=(), kind=jnp.bfloat16):
    level = level_of(rng, extent, cuts, -0.22, 0.18) if cuts else 1.0
    result = jax.random.normal(rng, extent, jnp.float32) * spread * level
    return jnp.minimum(jnp.maximum(result, -bound), bound).astype(kind)


def setup_inputs(seed: int = 0) -> dict:
    seeds = jax.random.split(jax.random.key(seed), 3)
    return {
        "kkt": draw_kkt(jax.random.fold_in(seeds[2], 71), 0),
        "directions": gaussian(seeds[1], (N, M), 1.0, 6.0, ((0, 8), (1, 4)), jnp.float32),
    }


def eliminated_through(positions, step_index):
    return (positions % STRIDE < NB) & (positions // STRIDE <= step_index)

def reference(kkt, directions):
    positions = jnp.arange(N, dtype=jnp.int32)
    schur = kkt
    solved = directions
    block_size = math.gcd(N, 1024)
    block_count = N // block_size
    for step_index in range(PANELS):
        first_index = step_index * STRIDE
        panel_cols = schur[:, first_index:first_index + NB]
        pivot_factor = jnp.linalg.cholesky(panel_cols[first_index:first_index + NB])
        solution_rows = jax.scipy.linalg.solve_triangular(pivot_factor, solved[first_index:first_index + NB], lower=True)
        panel_factor = jax.scipy.linalg.solve_triangular(pivot_factor, panel_cols.T, lower=True).T
        earlier_rows = eliminated_through(positions, step_index - 1)
        panel_factor = jnp.where(earlier_rows[:, None], 0.0, panel_factor)
        solved = solved - jnp.dot(panel_factor, solution_rows, precision=lax.Precision.HIGHEST)
        solved = solved.at[first_index:first_index + NB].set(solution_rows)
        kept = jnp.logical_not(eliminated_through(positions, step_index))
        factor_transposed = panel_factor.T

        def update_rows(pieces):
            rows_of_schur, rows_of_factor, rows_kept = pieces
            product = jnp.dot(rows_of_factor, factor_transposed, precision=lax.Precision.HIGHEST)
            return jnp.where(rows_kept[:, None] & kept[None, :], rows_of_schur - product, 0.0)
        schur = lax.map(update_rows, (schur.reshape(block_count, block_size, N), panel_factor.reshape(block_count, block_size, NB), kept.reshape(block_count, block_size))).reshape(N, N)
    return (schur, solved)
```

```python
import functools

import jax
import jax.numpy as jnp
from jax import lax
from jax.experimental import pallas as pl
from jax.experimental.pallas import tpu as pltpu
from jax.sharding import PartitionSpec as P

NB = 128
PANELS = 3
NJ = NB * PANELS
HIGHEST = lax.Precision.HIGHEST


def mm(a, b):
    return lax.dot_general(
        a, b, (((1,), (0,)), ((), ())), precision=HIGHEST, preferred_element_type=jnp.float32
    )


def mm_t(a, b):
    return lax.dot_general(
        a, b, (((1,), (1,)), ((), ())), precision=HIGHEST, preferred_element_type=jnp.float32
    )


def block_inverse_factor(block):
    row_ids = lax.broadcasted_iota(jnp.int32, (NB, NB), 0)
    lane_ids = lax.broadcasted_iota(jnp.int32, (NB, NB), 1)
    eye = jnp.where(row_ids == lane_ids, 1.0, 0.0).astype(jnp.float32)

    def step(j, state):
        a, w = state
        column = jnp.sum(jnp.where(lane_ids == j, a, 0.0), axis=1, keepdims=True)
        at_row = row_ids == j
        row_a = jnp.sum(jnp.where(at_row, a, 0.0), axis=0, keepdims=True)
        row_w = jnp.sum(jnp.where(at_row, w, 0.0), axis=0, keepdims=True)
        pivot = jnp.sum(jnp.where(at_row[:, :1], column, 0.0), axis=0, keepdims=True)
        scale = lax.rsqrt(pivot)
        scale = scale * (1.5 - 0.5 * pivot * scale * scale)
        row_a = row_a * scale
        row_w = row_w * scale
        factor = column * scale
        below = row_ids[:, :1] > j
        factor = jnp.where(below, factor, 0.0)
        a = a - factor * row_a
        w = jnp.where(at_row, row_w, w - factor * row_w)
        return (a, w)

    return lax.fori_loop(0, NB, step, (block, eye))[1]


def factor_inverse(m_ref, w_ref):
    part = lambda i: slice(i * NB, (i + 1) * NB)
    blocks = {}
    inverse = {}
    low = {}
    for i in range(PANELS):
        for j in range(i + 1):
            blocks[i, j] = m_ref[part(i), part(j)]
    for k in range(PANELS):
        inverse[k, k] = block_inverse_factor(blocks[k, k])
        for i in range(k + 1, PANELS):
            low[i, k] = mm_t(blocks[i, k], inverse[k, k])
        for i in range(k + 1, PANELS):
            for j in range(k + 1, i + 1):
                blocks[i, j] = blocks[i, j] - mm_t(low[i, k], low[j, k])
        for j in range(k):
            total = mm(low[k, j], inverse[j, j])
            for m in range(j + 1, k):
                total = total + mm(low[k, m], inverse[m, j])
            inverse[k, j] = -mm(inverse[k, k], total)
    for i in range(PANELS):
        for j in range(PANELS):
            w_ref[part(i), part(j)] = (
                inverse[i, j] if j <= i else jnp.zeros((NB, NB), jnp.float32)
            )


def pivot_kernel(m_ref, w_ref):
    factor_inverse(m_ref, w_ref)


def split(x):
    high = lax.reduce_precision(x, 8, 7)
    return high.astype(jnp.bfloat16), (x - high).astype(jnp.bfloat16)


def update_kernel(stride, row_count, place_ref, s_ref, y_ref, left_ref, right_ref, x_ref, so_ref, yo_ref):
    step = pl.program_id(0)
    col_count = s_ref.shape[1]
    left = left_ref[...]
    tile = min(1024, col_count)
    for start in range(0, col_count, tile):
        columns = slice(start, start + tile)
        so_ref[:, columns] = s_ref[:, columns] - jnp.dot(
            left, right_ref[:, columns], preferred_element_type=jnp.float32
        )
    yo_ref[...] = y_ref[...] - jnp.dot(
        left, right_ref[:, col_count:], preferred_element_type=jnp.float32
    )
    first_row = place_ref[0] * row_count
    first_col = place_ref[1] * col_count

    @pl.when((lax.rem(first_col, stride) == 0) & (first_col < PANELS * stride))
    def _():
        so_ref[:, :NB] = jnp.zeros((so_ref.shape[0], NB), jnp.float32)

    @pl.when((step == 0) & (lax.rem(first_row, stride) == 0) & (first_row < PANELS * stride))
    def _():
        so_ref[:NB, :] = jnp.zeros((NB, col_count), jnp.float32)
        k = lax.div(first_row, stride)
        yo_ref[:NB, :] = x_ref[pl.ds(pl.multiple_of(k * NB, NB), NB), :]


def update(kkt, directions, row_panel, col_panel, x, place, stride):
    row_count, col_count = kkt.shape
    width = directions.shape[1]
    rows = min(256, row_count)
    depth = row_panel.shape[1]
    whole = lambda i, place: (0, 0)
    tiles = lambda i, place: (i, 0)
    return pl.pallas_call(
        functools.partial(update_kernel, stride, row_count),
        out_shape=(
            jax.ShapeDtypeStruct(kkt.shape, jnp.float32),
            jax.ShapeDtypeStruct(directions.shape, jnp.float32),
        ),
        grid_spec=pltpu.PrefetchScalarGridSpec(
            num_scalar_prefetch=1,
            grid=(row_count // rows,),
            in_specs=[
                pl.BlockSpec((rows, col_count), tiles),
                pl.BlockSpec((rows, width), tiles),
                pl.BlockSpec((rows, depth), tiles),
                pl.BlockSpec((depth, col_count + width), whole),
                pl.BlockSpec((NJ, width), whole),
            ],
            out_specs=[
                pl.BlockSpec((rows, col_count), tiles),
                pl.BlockSpec((rows, width), tiles),
            ],
        ),
        compiler_params=pltpu.CompilerParams(vmem_limit_bytes=56 * 2**20),
        cost_estimate=pl.CostEstimate(
            flops=2 * row_count * (col_count + width) * depth,
            bytes_accessed=8 * row_count * (col_count + width),
            transcendentals=0,
        ),
    )(place, kkt, directions, row_panel, col_panel, x)


def on_device(kkt, directions):
    row_count, col_count = kkt.shape
    order_total = row_count * lax.axis_size("row")
    stride = order_total // (PANELS + 1)
    assert stride % row_count == 0 and stride % col_count == 0
    row_index = lax.axis_index("row")
    col_index = lax.axis_index(("grp", "col"))
    row_owner = [k * stride // row_count for k in range(PANELS)]
    col_owner = [k * stride // col_count for k in range(PANELS)]

    own_cols = kkt[:, :NB]
    own_rows = jnp.concatenate([kkt[:NB], directions[:NB]], axis=1)
    row_panel = jnp.concatenate(
        [jnp.where(col_index == owner, own_cols, 0.0) for owner in col_owner], axis=1
    )
    row_panel = lax.psum(row_panel, ("grp", "col"))
    pivot = jnp.concatenate(
        [jnp.where(row_index == owner, row_panel[:NB], 0.0) for owner in row_owner], axis=0
    )
    col_panel = jnp.concatenate(
        [jnp.where(row_index == owner, own_rows, 0.0) for owner in row_owner], axis=0
    )
    pivot = lax.psum(pivot, "row")
    col_panel = lax.psum(col_panel, "row")
    inverse = pl.pallas_call(
        pivot_kernel,
        out_shape=jax.ShapeDtypeStruct((NJ, NJ), jnp.float32),
        compiler_params=pltpu.CompilerParams(vmem_limit_bytes=32 * 2**20),
    )(pivot)
    row_factor = mm_t(row_panel, inverse)
    col_factor = mm(inverse, col_panel)
    row_high, row_low = split(row_factor)
    col_high, col_low = split(col_factor)
    left = jnp.concatenate([row_high, row_low, row_high], axis=1)
    right = jnp.concatenate([col_high, col_high, col_low], axis=0)
    place = jnp.stack([row_index, col_index]).astype(jnp.int32)
    return update(kkt, directions, left, right, col_factor[:, col_count:], place, stride)


def solution(mesh):
    specs = (P("row", ("grp", "col")), P("row", ("grp", "col")))
    return jax.shard_map(
        on_device, mesh=mesh, in_specs=specs, out_specs=specs, check_vma=False
    )
```

```python
import functools

import jax
import jax.numpy as jnp
from jax import lax
from jax.experimental import pallas as pl
from jax.experimental.pallas import tpu as pltpu
from jax.sharding import PartitionSpec as P

NB = 128
PANELS = 3
NJ = NB * PANELS
HIGHEST = lax.Precision.HIGHEST


def mm(a, b):
    return lax.dot_general(
        a, b, (((1,), (0,)), ((), ())), precision=HIGHEST, preferred_element_type=jnp.float32
    )


def mm_t(a, b):
    return lax.dot_general(
        a, b, (((1,), (1,)), ((), ())), precision=HIGHEST, preferred_element_type=jnp.float32
    )


def block_inverse_factor(block):
    row_ids = lax.broadcasted_iota(jnp.int32, (NB, NB), 0)
    lane_ids = lax.broadcasted_iota(jnp.int32, (NB, NB), 1)
    eye = jnp.where(row_ids == lane_ids, 1.0, 0.0).astype(jnp.float32)

    def step(j, state):
        a, w = state
        column = jnp.sum(jnp.where(lane_ids == j, a, 0.0), axis=1, keepdims=True)
        at_row = row_ids == j
        row_a = jnp.sum(jnp.where(at_row, a, 0.0), axis=0, keepdims=True)
        row_w = jnp.sum(jnp.where(at_row, w, 0.0), axis=0, keepdims=True)
        pivot = jnp.sum(jnp.where(at_row[:, :1], column, 0.0), axis=0, keepdims=True)
        scale = lax.rsqrt(pivot)
        scale = scale * (1.5 - 0.5 * pivot * scale * scale)
        row_a = row_a * scale
        row_w = row_w * scale
        factor = column * scale
        below = row_ids[:, :1] > j
        factor = jnp.where(below, factor, 0.0)
        a = a - factor * row_a
        w = jnp.where(at_row, row_w, w - factor * row_w)
        return (a, w)

    return lax.fori_loop(0, NB, step, (block, eye))[1]


def factor_inverse(m_ref, w_ref):
    part = lambda i: slice(i * NB, (i + 1) * NB)
    blocks = {}
    inverse = {}
    low = {}
    for i in range(PANELS):
        for j in range(i + 1):
            blocks[i, j] = m_ref[part(i), part(j)]
    for k in range(PANELS):
        inverse[k, k] = block_inverse_factor(blocks[k, k])
        for i in range(k + 1, PANELS):
            low[i, k] = mm_t(blocks[i, k], inverse[k, k])
        for i in range(k + 1, PANELS):
            for j in range(k + 1, i + 1):
                blocks[i, j] = blocks[i, j] - mm_t(low[i, k], low[j, k])
        for j in range(k):
            total = mm(low[k, j], inverse[j, j])
            for m in range(j + 1, k):
                total = total + mm(low[k, m], inverse[m, j])
            inverse[k, j] = -mm(inverse[k, k], total)
    for i in range(PANELS):
        for j in range(PANELS):
            w_ref[part(i), part(j)] = (
                inverse[i, j] if j <= i else jnp.zeros((NB, NB), jnp.float32)
            )


def pivot_kernel(m_ref, w_ref):
    factor_inverse(m_ref, w_ref)


def split(x):
    high = lax.reduce_precision(x, 8, 7)
    return high.astype(jnp.bfloat16), (x - high).astype(jnp.bfloat16)


def update_kernel(stride, row_count, place_ref, s_ref, y_ref, left_ref, right_ref, x_ref, so_ref, yo_ref):
    step = pl.program_id(0)
    col_count = s_ref.shape[1]
    left = left_ref[...]
    tile = min(1024, col_count)
    for start in range(0, col_count, tile):
        columns = slice(start, start + tile)
        so_ref[:, columns] = s_ref[:, columns] - jnp.dot(
            left, right_ref[:, columns], preferred_element_type=jnp.float32
        )
    yo_ref[...] = y_ref[...] - jnp.dot(
        left, right_ref[:, col_count:], preferred_element_type=jnp.float32
    )
    first_row = place_ref[0] * row_count
    first_col = place_ref[1] * col_count

    @pl.when((lax.rem(first_col, stride) == 0) & (first_col < PANELS * stride))
    def _():
        so_ref[:, :NB] = jnp.zeros((so_ref.shape[0], NB), jnp.float32)

    @pl.when((step == 0) & (lax.rem(first_row, stride) == 0) & (first_row < PANELS * stride))
    def _():
        so_ref[:NB, :] = jnp.zeros((NB, col_count), jnp.float32)
        k = lax.div(first_row, stride)
        yo_ref[:NB, :] = x_ref[pl.ds(pl.multiple_of(k * NB, NB), NB), :]


def update(kkt, directions, row_panel, col_panel, x, place, stride):
    row_count, col_count = kkt.shape
    width = directions.shape[1]
    rows = min(256, row_count)
    depth = row_panel.shape[1]
    whole = lambda i, place: (0, 0)
    tiles = lambda i, place: (i, 0)
    return pl.pallas_call(
        functools.partial(update_kernel, stride, row_count),
        out_shape=(
            jax.ShapeDtypeStruct(kkt.shape, jnp.float32),
            jax.ShapeDtypeStruct(directions.shape, jnp.float32),
        ),
        grid_spec=pltpu.PrefetchScalarGridSpec(
            num_scalar_prefetch=1,
            grid=(row_count // rows,),
            in_specs=[
                pl.BlockSpec((rows, col_count), tiles),
                pl.BlockSpec((rows, width), tiles),
                pl.BlockSpec((rows, depth), tiles),
                pl.BlockSpec((depth, col_count + width), whole),
                pl.BlockSpec((NJ, width), whole),
            ],
            out_specs=[
                pl.BlockSpec((rows, col_count), tiles),
                pl.BlockSpec((rows, width), tiles),
            ],
        ),
        compiler_params=pltpu.CompilerParams(vmem_limit_bytes=56 * 2**20),
        cost_estimate=pl.CostEstimate(
            flops=2 * row_count * (col_count + width) * depth,
            bytes_accessed=8 * row_count * (col_count + width),
            transcendentals=0,
        ),
    )(place, kkt, directions, row_panel, col_panel, x)


CHUNKS = 4
STEPS = PANELS * CHUNKS


def gather_kernel(
    cols_ref, y_ref, row_buf, col_buf, m_buf, y_buf,
    near_recv, x_send, core_send, z_recv, up_send, down_send, side_recv, side_send,
    m_send, m_recv, y_send, y_recv,
):
    g, row, x = lax.axis_index("grp"), lax.axis_index("row"), lax.axis_index("col")
    z, y = row // 2, row % 2
    source = 2 * g + x
    size = cols_ref.shape[0] // CHUNKS
    core = (1 - g, row, x)
    across = (g, row, 1 - x)
    side = (g, z * 2 + 1 - y, x)
    peers = [(g, lax.rem(row + 1 + p, 8), x) for p in range(7)]

    barrier = pltpu.get_barrier_semaphore()
    for target in [core, across] + peers:
        pl.semaphore_signal(barrier, inc=1, device_id=target, device_id_type=pl.DeviceIdType.MESH)
    pl.semaphore_wait(barrier, 9)

    def remote(src, dst, send, recv, target):
        return pltpu.make_async_remote_copy(
            src_ref=src, dst_ref=dst, send_sem=send, recv_sem=recv,
            device_id=target, device_id_type=pl.DeviceIdType.MESH,
        )

    def place(i):
        k = i // CHUNKS
        start = pl.multiple_of((i % CHUNKS) * size, size)
        owner_g = jnp.where(k == 2, 1, 0)
        owner_x = jnp.where(k == 1, 1, 0)
        return k, pl.ds(start, size), g == owner_g, x == owner_x

    def near(i, send, target):
        k, rows, _, _ = place(i)
        ref = row_buf.at[k, rows]
        return remote(ref, ref, send.at[i], near_recv.at[i], target)

    def far(i, from_y, send, recv, target):
        k, rows, _, _ = place(i)
        ref = col_buf.at[from_y, k, rows]
        return remote(ref, ref, send.at[i], recv.at[i], target)

    up = (g, lax.rem(row + 2, 8), x)
    down = (g, lax.rem(row + 6, 8), x)
    goes_up = (z >= source) & (z < 3)
    goes_down = (z <= source) & (z > 0)
    is_owner = (y == 0) & (z < 3)

    @pl.when(is_owner)
    def _():
        for p in range(7):
            remote(y_ref, y_buf.at[z], y_send.at[p], y_recv.at[z], peers[p]).start()
        y_buf[z] = y_ref[...]

    @pl.loop(0, STEPS)
    def _(i):
        k, rows, same_g, same_x = place(i)

        @pl.when(same_g & same_x)
        def _():
            row_buf[k, rows] = cols_ref[rows]
            near(i, x_send, across).start()
            near(i, core_send, core).start()

    def near_step(i):
        _, _, same_g, same_x = place(i)

        @pl.when(jnp.logical_not(same_g & same_x))
        def _():
            near(i, x_send, across).wait_recv()

        @pl.when(same_g & jnp.logical_not(same_x))
        def _():
            near(i, core_send, core).start()

    def far_step(i):
        k, rows, _, _ = place(i)

        @pl.when(z == source)
        def _():
            col_buf[y, k, rows] = row_buf[k, rows]

        @pl.when(z != source)
        def _():
            far(i, y, up_send, z_recv, up).wait_recv()

        @pl.when(goes_up)
        def _():
            far(i, y, up_send, z_recv, up).start()

        @pl.when(goes_down)
        def _():
            far(i, y, down_send, z_recv, down).start()

        far(i, y, side_send, side_recv, side).start()

    @pl.loop(0, CHUNKS)
    def _(i):
        near_step(i)

    @pl.loop(0, STEPS - CHUNKS)
    def _(i):
        near_step(i + CHUNKS)
        far_step(i)

    head = row_buf.at[:, pl.ds(0, NB)]

    @pl.when(is_owner)
    def _():
        for p in range(7):
            remote(head, m_buf.at[z], m_send.at[p], m_recv.at[z], peers[p]).start()
        m_buf[z] = head[...]

    @pl.loop(STEPS - CHUNKS, STEPS)
    def _(i):
        far_step(i)

    for j in range(PANELS):
        @pl.when(row != 2 * j)
        def _():
            remote(y_ref, y_buf.at[j], y_send.at[0], y_recv.at[j], peers[0]).wait_recv()
            remote(head, m_buf.at[j], m_send.at[0], m_recv.at[j], peers[0]).wait_recv()

    @pl.when(is_owner)
    def _():
        for p in range(7):
            remote(y_ref, y_buf.at[z], y_send.at[p], y_recv.at[z], peers[p]).wait_send()
            remote(head, m_buf.at[z], m_send.at[p], m_recv.at[z], peers[p]).wait_send()

    @pl.loop(0, STEPS)
    def _(i):
        _, _, same_g, same_x = place(i)
        far(i, 1 - y, side_send, side_recv, side).wait_recv()
        far(i, y, side_send, side_recv, side).wait_send()

        @pl.when(goes_up)
        def _():
            far(i, y, up_send, z_recv, up).wait_send()

        @pl.when(goes_down)
        def _():
            far(i, y, down_send, z_recv, down).wait_send()

        @pl.when(same_g)
        def _():
            near(i, core_send, core).wait_send()

        @pl.when(same_g & same_x)
        def _():
            near(i, x_send, across).wait_send()


def gather(own_cols, own_y):
    count, width = own_cols.shape[0], own_y.shape[1]
    vmem = pl.BlockSpec(memory_space=pltpu.VMEM)
    shapes = [(PANELS, count, NB), (2, PANELS, count, NB), (PANELS, PANELS, NB, NB), (PANELS, NB, width)]
    counts = [STEPS] * 8 + [7, PANELS, 7, PANELS]
    return pl.pallas_call(
        gather_kernel,
        out_shape=[jax.ShapeDtypeStruct(shape, jnp.float32) for shape in shapes],
        in_specs=[vmem, vmem],
        out_specs=[vmem] * 4,
        scratch_shapes=[pltpu.SemaphoreType.DMA((n,)) for n in counts],
        compiler_params=pltpu.CompilerParams(
            collective_id=0, has_side_effects=True, vmem_limit_bytes=32 * 2**20
        ),
    )(own_cols, own_y)


def on_device(kkt, directions):
    row_count, col_count = kkt.shape
    order_total = row_count * lax.axis_size("row")
    stride = order_total // (PANELS + 1)
    assert stride % row_count == 0 and stride % col_count == 0
    row_index = lax.axis_index("row")
    col_index = lax.axis_index(("grp", "col"))
    row_owner = [k * stride // row_count for k in range(PANELS)]
    col_owner = [k * stride // col_count for k in range(PANELS)]

    near_shape = tuple(lax.axis_size(a) for a in ("grp", "row", "col")) == (2, 8, 2)
    if near_shape and col_count == 2 * row_count:
        row_buf, col_buf, m_buf, y_buf = gather(kkt[:, :NB], directions[:NB])
        row_panel = row_buf.transpose(1, 0, 2).reshape(row_count, NJ)
        pivot = m_buf.transpose(0, 2, 1, 3).reshape(NJ, NJ)
        col_rows = col_buf.transpose(0, 2, 1, 3).reshape(col_count, NJ)
        col_panel = None
    else:
        own_cols = kkt[:, :NB]
        own_rows = jnp.concatenate([kkt[:NB], directions[:NB]], axis=1)
        row_panel = jnp.concatenate(
            [jnp.where(col_index == owner, own_cols, 0.0) for owner in col_owner], axis=1
        )
        row_panel = lax.psum(row_panel, ("grp", "col"))
        pivot = jnp.concatenate(
            [jnp.where(row_index == owner, row_panel[:NB], 0.0) for owner in row_owner], axis=0
        )
        col_panel = jnp.concatenate(
            [jnp.where(row_index == owner, own_rows, 0.0) for owner in row_owner], axis=0
        )
        pivot = lax.psum(pivot, "row")
        col_panel = lax.psum(col_panel, "row")
    inverse = pl.pallas_call(
        pivot_kernel,
        out_shape=jax.ShapeDtypeStruct((NJ, NJ), jnp.float32),
        compiler_params=pltpu.CompilerParams(vmem_limit_bytes=32 * 2**20),
    )(pivot)
    row_factor = mm_t(row_panel, inverse)
    if col_panel is None:
        col_factor = jnp.concatenate(
            [mm_t(inverse, col_rows), mm(inverse, y_buf.reshape(NJ, -1))], axis=1
        )
    else:
        col_factor = mm(inverse, col_panel)
    row_high, row_low = split(row_factor)
    col_high, col_low = split(col_factor)
    left = jnp.concatenate([row_high, row_low, row_high], axis=1)
    right = jnp.concatenate([col_high, col_high, col_low], axis=0)
    place = jnp.stack([row_index, col_index]).astype(jnp.int32)
    return update(kkt, directions, left, right, col_factor[:, col_count:], place, stride)


def solution(mesh):
    specs = (P("row", ("grp", "col")), P("row", ("grp", "col")))
    return jax.shard_map(
        on_device, mesh=mesh, in_specs=specs, out_specs=specs, check_vma=False
    )
```

```python
import functools

import jax
import jax.numpy as jnp
from jax import lax
from jax.experimental import pallas as pl
from jax.experimental.pallas import tpu as pltpu
from jax.sharding import PartitionSpec as P

NB = 128
PANELS = 3
NJ = NB * PANELS
HIGHEST = lax.Precision.HIGHEST


def mm(a, b):
    return lax.dot_general(
        a, b, (((1,), (0,)), ((), ())), precision=HIGHEST, preferred_element_type=jnp.float32
    )


def mm_t(a, b):
    return lax.dot_general(
        a, b, (((1,), (1,)), ((), ())), precision=HIGHEST, preferred_element_type=jnp.float32
    )


def block_inverse_factor(block):
    row_ids = lax.broadcasted_iota(jnp.int32, (NB, NB), 0)
    lane_ids = lax.broadcasted_iota(jnp.int32, (NB, NB), 1)
    eye = jnp.where(row_ids == lane_ids, 1.0, 0.0).astype(jnp.float32)

    def step(j, state):
        a, w = state
        column = jnp.sum(jnp.where(lane_ids == j, a, 0.0), axis=1, keepdims=True)
        at_row = row_ids == j
        row_a = jnp.sum(jnp.where(at_row, a, 0.0), axis=0, keepdims=True)
        row_w = jnp.sum(jnp.where(at_row, w, 0.0), axis=0, keepdims=True)
        pivot = jnp.sum(jnp.where(at_row[:, :1], column, 0.0), axis=0, keepdims=True)
        scale = lax.rsqrt(pivot)
        scale = scale * (1.5 - 0.5 * pivot * scale * scale)
        row_a = row_a * scale
        row_w = row_w * scale
        factor = column * scale
        below = row_ids[:, :1] > j
        factor = jnp.where(below, factor, 0.0)
        a = a - factor * row_a
        w = jnp.where(at_row, row_w, w - factor * row_w)
        return (a, w)

    return lax.fori_loop(0, NB, step, (block, eye))[1]


def factor_inverse(m_ref, w_ref):
    part = lambda i: slice(i * NB, (i + 1) * NB)
    blocks = {}
    inverse = {}
    low = {}
    for i in range(PANELS):
        for j in range(i + 1):
            blocks[i, j] = m_ref[part(i), part(j)]
    for k in range(PANELS):
        inverse[k, k] = block_inverse_factor(blocks[k, k])
        for i in range(k + 1, PANELS):
            low[i, k] = mm_t(blocks[i, k], inverse[k, k])
        for i in range(k + 1, PANELS):
            for j in range(k + 1, i + 1):
                blocks[i, j] = blocks[i, j] - mm_t(low[i, k], low[j, k])
        for j in range(k):
            total = mm(low[k, j], inverse[j, j])
            for m in range(j + 1, k):
                total = total + mm(low[k, m], inverse[m, j])
            inverse[k, j] = -mm(inverse[k, k], total)
    for i in range(PANELS):
        for j in range(PANELS):
            w_ref[part(i), part(j)] = (
                inverse[i, j] if j <= i else jnp.zeros((NB, NB), jnp.float32)
            )


def pivot_kernel(m_ref, w_ref):
    factor_inverse(m_ref, w_ref)


def factor_kernel(row_buf, col_buf, m_buf, y_buf, left_ref, right_ref, x_ref, m_ref, w_ref):
    count = row_buf.shape[1]
    tile = 512
    part = lambda k: slice(k * NB, (k + 1) * NB)
    for j in range(PANELS):
        for k in range(PANELS):
            m_ref[part(j), part(k)] = m_buf[j, k]
    factor_inverse(m_ref, w_ref)

    def put_right(columns, value):
        high = value.astype(jnp.bfloat16)
        right_ref[:NJ, columns] = high
        right_ref[NJ:2 * NJ, columns] = high
        right_ref[2 * NJ:, columns] = (value - high.astype(jnp.float32)).astype(jnp.bfloat16)

    @pl.loop(0, count // tile)
    def _(i):
        start = pl.multiple_of(i * tile, tile)
        rows = pl.ds(start, tile)
        own = jnp.concatenate([row_buf[k, rows] for k in range(PANELS)], axis=1)
        value = mm_t(own, w_ref[...])
        high = value.astype(jnp.bfloat16)
        left_ref[rows, :NJ] = high
        left_ref[rows, NJ:2 * NJ] = (value - high.astype(jnp.float32)).astype(jnp.bfloat16)
        left_ref[rows, 2 * NJ:] = high
        for side in range(2):
            across = jnp.concatenate([col_buf[side, k, rows] for k in range(PANELS)], axis=1)
            columns = pl.ds(pl.multiple_of(side * count + start, tile), tile)
            put_right(columns, mm_t(w_ref[...], across))

    x = mm(w_ref[...], jnp.concatenate([y_buf[k] for k in range(PANELS)], axis=0))
    x_ref[...] = x
    put_right(slice(2 * count, 2 * count + x.shape[1]), x)


def factor(row_buf, col_buf, m_buf, y_buf):
    count, width = row_buf.shape[1], y_buf.shape[2]
    vmem = pl.BlockSpec(memory_space=pltpu.VMEM)
    return pl.pallas_call(
        factor_kernel,
        out_shape=[
            jax.ShapeDtypeStruct((count, 3 * NJ), jnp.bfloat16),
            jax.ShapeDtypeStruct((3 * NJ, 2 * count + width), jnp.bfloat16),
            jax.ShapeDtypeStruct((NJ, width), jnp.float32),
        ],
        in_specs=[vmem] * 4,
        out_specs=[vmem] * 3,
        scratch_shapes=[pltpu.VMEM((NJ, NJ), jnp.float32)] * 2,
        compiler_params=pltpu.CompilerParams(vmem_limit_bytes=50 * 2**20),
    )(row_buf, col_buf, m_buf, y_buf)


def split(x):
    high = lax.reduce_precision(x, 8, 7)
    return high.astype(jnp.bfloat16), (x - high).astype(jnp.bfloat16)


def update_kernel(stride, row_count, place_ref, s_ref, y_ref, left_ref, right_ref, x_ref, so_ref, yo_ref):
    step = pl.program_id(0)
    col_count = s_ref.shape[1]
    left = left_ref[...]
    tile = min(1024, col_count)
    for start in range(0, col_count, tile):
        columns = slice(start, start + tile)
        so_ref[:, columns] = s_ref[:, columns] - jnp.dot(
            left, right_ref[:, columns], preferred_element_type=jnp.float32
        )
    yo_ref[...] = y_ref[...] - jnp.dot(
        left, right_ref[:, col_count:], preferred_element_type=jnp.float32
    )
    first_row = place_ref[0] * row_count
    first_col = place_ref[1] * col_count

    @pl.when((lax.rem(first_col, stride) == 0) & (first_col < PANELS * stride))
    def _():
        so_ref[:, :NB] = jnp.zeros((so_ref.shape[0], NB), jnp.float32)

    @pl.when((step == 0) & (lax.rem(first_row, stride) == 0) & (first_row < PANELS * stride))
    def _():
        so_ref[:NB, :] = jnp.zeros((NB, col_count), jnp.float32)
        k = lax.div(first_row, stride)
        yo_ref[:NB, :] = x_ref[pl.ds(pl.multiple_of(k * NB, NB), NB), :]


def update(kkt, directions, row_panel, col_panel, x, place, stride):
    row_count, col_count = kkt.shape
    width = directions.shape[1]
    rows = min(256, row_count)
    depth = row_panel.shape[1]
    whole = lambda i, place: (0, 0)
    tiles = lambda i, place: (i, 0)
    return pl.pallas_call(
        functools.partial(update_kernel, stride, row_count),
        out_shape=(
            jax.ShapeDtypeStruct(kkt.shape, jnp.float32),
            jax.ShapeDtypeStruct(directions.shape, jnp.float32),
        ),
        grid_spec=pltpu.PrefetchScalarGridSpec(
            num_scalar_prefetch=1,
            grid=(row_count // rows,),
            in_specs=[
                pl.BlockSpec((rows, col_count), tiles),
                pl.BlockSpec((rows, width), tiles),
                pl.BlockSpec((rows, depth), tiles),
                pl.BlockSpec((depth, col_count + width), whole),
                pl.BlockSpec((NJ, width), whole),
            ],
            out_specs=[
                pl.BlockSpec((rows, col_count), tiles),
                pl.BlockSpec((rows, width), tiles),
            ],
        ),
        compiler_params=pltpu.CompilerParams(vmem_limit_bytes=56 * 2**20),
        cost_estimate=pl.CostEstimate(
            flops=2 * row_count * (col_count + width) * depth,
            bytes_accessed=8 * row_count * (col_count + width),
            transcendentals=0,
        ),
    )(place, kkt, directions, row_panel, col_panel, x)


CHUNKS = 4
STEPS = PANELS * CHUNKS


def gather_kernel(
    cols_ref, y_ref, row_buf, col_buf, m_buf, y_buf,
    near_recv, x_send, core_send, z_recv, up_send, down_send, side_recv, side_send,
    m_send, m_recv, y_send, y_recv,
):
    g, row, x = lax.axis_index("grp"), lax.axis_index("row"), lax.axis_index("col")
    z, y = row // 2, row % 2
    source = 2 * g + x
    size = cols_ref.shape[0] // CHUNKS
    core = (1 - g, row, x)
    across = (g, row, 1 - x)
    side = (g, z * 2 + 1 - y, x)
    peers = [(g, lax.rem(row + 1 + p, 8), x) for p in range(7)]

    barrier = pltpu.get_barrier_semaphore()
    for target in [core, across] + peers:
        pl.semaphore_signal(barrier, inc=1, device_id=target, device_id_type=pl.DeviceIdType.MESH)
    pl.semaphore_wait(barrier, 9)

    def remote(src, dst, send, recv, target):
        return pltpu.make_async_remote_copy(
            src_ref=src, dst_ref=dst, send_sem=send, recv_sem=recv,
            device_id=target, device_id_type=pl.DeviceIdType.MESH,
        )

    def place(i):
        k = i // CHUNKS
        start = pl.multiple_of((i % CHUNKS) * size, size)
        owner_g = jnp.where(k == 2, 1, 0)
        owner_x = jnp.where(k == 1, 1, 0)
        return k, pl.ds(start, size), g == owner_g, x == owner_x

    def near(i, send, target):
        k, rows, _, _ = place(i)
        ref = row_buf.at[k, rows]
        return remote(ref, ref, send.at[i], near_recv.at[i], target)

    def far(i, from_y, send, recv, target):
        k, rows, _, _ = place(i)
        ref = col_buf.at[from_y, k, rows]
        return remote(ref, ref, send.at[i], recv.at[i], target)

    up = (g, lax.rem(row + 2, 8), x)
    down = (g, lax.rem(row + 6, 8), x)
    goes_up = (z >= source) & (z < 3)
    goes_down = (z <= source) & (z > 0)
    is_owner = (y == 0) & (z < 3)

    @pl.when(is_owner)
    def _():
        for p in range(7):
            remote(y_ref, y_buf.at[z], y_send.at[p], y_recv.at[z], peers[p]).start()
        y_buf[z] = y_ref[...]

    @pl.loop(0, STEPS)
    def _(i):
        k, rows, same_g, same_x = place(i)

        @pl.when(same_g & same_x)
        def _():
            row_buf[k, rows] = cols_ref[rows]
            near(i, x_send, across).start()
            near(i, core_send, core).start()

    def near_step(i):
        _, _, same_g, same_x = place(i)

        @pl.when(jnp.logical_not(same_g & same_x))
        def _():
            near(i, x_send, across).wait_recv()

        @pl.when(same_g & jnp.logical_not(same_x))
        def _():
            near(i, core_send, core).start()

    def far_step(i):
        k, rows, _, _ = place(i)

        @pl.when(z == source)
        def _():
            col_buf[y, k, rows] = row_buf[k, rows]

        @pl.when(z != source)
        def _():
            far(i, y, up_send, z_recv, up).wait_recv()

        @pl.when(goes_up)
        def _():
            far(i, y, up_send, z_recv, up).start()

        @pl.when(goes_down)
        def _():
            far(i, y, down_send, z_recv, down).start()

        far(i, y, side_send, side_recv, side).start()

    @pl.loop(0, CHUNKS)
    def _(i):
        near_step(i)

    @pl.loop(0, STEPS - CHUNKS)
    def _(i):
        near_step(i + CHUNKS)
        far_step(i)

    head = row_buf.at[:, pl.ds(0, NB)]

    @pl.when(is_owner)
    def _():
        for p in range(7):
            remote(head, m_buf.at[z], m_send.at[p], m_recv.at[z], peers[p]).start()
        m_buf[z] = head[...]

    @pl.loop(STEPS - CHUNKS, STEPS)
    def _(i):
        far_step(i)

    for j in range(PANELS):
        @pl.when(row != 2 * j)
        def _():
            remote(y_ref, y_buf.at[j], y_send.at[0], y_recv.at[j], peers[0]).wait_recv()
            remote(head, m_buf.at[j], m_send.at[0], m_recv.at[j], peers[0]).wait_recv()

    @pl.when(is_owner)
    def _():
        for p in range(7):
            remote(y_ref, y_buf.at[z], y_send.at[p], y_recv.at[z], peers[p]).wait_send()
            remote(head, m_buf.at[z], m_send.at[p], m_recv.at[z], peers[p]).wait_send()

    @pl.loop(0, STEPS)
    def _(i):
        _, _, same_g, same_x = place(i)
        far(i, 1 - y, side_send, side_recv, side).wait_recv()
        far(i, y, side_send, side_recv, side).wait_send()

        @pl.when(goes_up)
        def _():
            far(i, y, up_send, z_recv, up).wait_send()

        @pl.when(goes_down)
        def _():
            far(i, y, down_send, z_recv, down).wait_send()

        @pl.when(same_g)
        def _():
            near(i, core_send, core).wait_send()

        @pl.when(same_g & same_x)
        def _():
            near(i, x_send, across).wait_send()


def gather(own_cols, own_y):
    count, width = own_cols.shape[0], own_y.shape[1]
    vmem = pl.BlockSpec(memory_space=pltpu.VMEM)
    shapes = [(PANELS, count, NB), (2, PANELS, count, NB), (PANELS, PANELS, NB, NB), (PANELS, NB, width)]
    counts = [STEPS] * 8 + [7, PANELS, 7, PANELS]
    return pl.pallas_call(
        gather_kernel,
        out_shape=[jax.ShapeDtypeStruct(shape, jnp.float32) for shape in shapes],
        in_specs=[vmem, vmem],
        out_specs=[vmem] * 4,
        scratch_shapes=[pltpu.SemaphoreType.DMA((n,)) for n in counts],
        compiler_params=pltpu.CompilerParams(
            collective_id=0, has_side_effects=True, vmem_limit_bytes=32 * 2**20
        ),
    )(own_cols, own_y)


def on_device(kkt, directions):
    row_count, col_count = kkt.shape
    order_total = row_count * lax.axis_size("row")
    stride = order_total // (PANELS + 1)
    assert stride % row_count == 0 and stride % col_count == 0
    row_index = lax.axis_index("row")
    col_index = lax.axis_index(("grp", "col"))
    row_owner = [k * stride // row_count for k in range(PANELS)]
    col_owner = [k * stride // col_count for k in range(PANELS)]

    place = jnp.stack([row_index, col_index]).astype(jnp.int32)
    near_shape = tuple(lax.axis_size(a) for a in ("grp", "row", "col")) == (2, 8, 2)
    if near_shape and col_count == 2 * row_count:
        row_buf, col_buf, m_buf, y_buf = gather(kkt[:, :NB], directions[:NB])
        left, right, x = factor(row_buf, col_buf, m_buf, y_buf)
        return update(kkt, directions, left, right, x, place, stride)

    own_cols = kkt[:, :NB]
    own_rows = jnp.concatenate([kkt[:NB], directions[:NB]], axis=1)
    row_panel = jnp.concatenate(
        [jnp.where(col_index == owner, own_cols, 0.0) for owner in col_owner], axis=1
    )
    row_panel = lax.psum(row_panel, ("grp", "col"))
    pivot = jnp.concatenate(
        [jnp.where(row_index == owner, row_panel[:NB], 0.0) for owner in row_owner], axis=0
    )
    col_panel = jnp.concatenate(
        [jnp.where(row_index == owner, own_rows, 0.0) for owner in row_owner], axis=0
    )
    pivot = lax.psum(pivot, "row")
    col_panel = lax.psum(col_panel, "row")
    inverse = pl.pallas_call(
        pivot_kernel,
        out_shape=jax.ShapeDtypeStruct((NJ, NJ), jnp.float32),
        compiler_params=pltpu.CompilerParams(vmem_limit_bytes=32 * 2**20),
    )(pivot)
    row_factor = mm_t(row_panel, inverse)
    col_factor = mm(inverse, col_panel)
    row_high, row_low = split(row_factor)
    col_high, col_low = split(col_factor)
    left = jnp.concatenate([row_high, row_low, row_high], axis=1)
    right = jnp.concatenate([col_high, col_high, col_low], axis=0)
    return update(kkt, directions, left, right, col_factor[:, col_count:], place, stride)


def solution(mesh):
    specs = (P("row", ("grp", "col")), P("row", ("grp", "col")))
    return jax.shard_map(
        on_device, mesh=mesh, in_specs=specs, out_specs=specs, check_vma=False
    )
```
